32 devices in a mesh: grp: 8 (over z, y), seq: 4 (over x, core).
Axes of the slice: x: 2, y: 2, z: 4, core: 2. Of those that a mesh axis runs over, the one named last changes fastest.
Arguments:
- slates: bfloat16 [8, 2048, 1024], P('grp', 'seq'), may hold values from -6 to 6
- owner: int32 [1], replicated, may hold values from 0 to 7
- hist_keys: bfloat16 [16, 1536, 1024], P('grp', 'seq'), may hold values from -6 to 6
- hist_values: bfloat16 [16, 1536, 1024], P('grp', 'seq'), may hold values from -6 to 6
- lengths: int32 [16], P('grp'), may hold values from 1 to 1536, 12288 in all
- proj_weight: bfloat16 [1024, 4, 1024], P(None, None, 'seq'), may hold values from -0.1875 to 0.1875
- out_weight: bfloat16 [1024, 1024], replicated, may hold values from -0.1875 to 0.1875
Outputs:
- scored: bfloat16 [16, 2048, 1024], P('grp', 'seq')
The draws below stay inside these ranges and needn't reach their ends.
Inputs may be any that keep to these rules, and one draw needn't show every extreme that they name: `lengths`: every user has at least one position; some user has all 1536.
All inputs are finite; a program needn't handle non-finite values. No bound on the sum of `lengths` on one device may be relied on, other than what follows from the above.
Results may differ from the reference program's by a relative error of at most 0.0053.
Values may be sent and summed in bfloat16 or wider, within the bound.
A program may use at most 128 MiB of HBM per device.

```python
import math
import jax
import jax.numpy as jnp
import numpy as np
from jax import lax

D = 1024
H = 16
NC = 2048
HIST = 1536
USERS = 16
N_GRP = 8


def shard_levels(stream_key, dims, split, low, top_value):
    def one(position, parts):
        steps = jax.random.uniform(jax.random.fold_in(jax.random.fold_in(stream_key, 6), position), (parts,), jnp.float32, low / len(split), top_value / len(split))
        return jnp.repeat(jnp.exp(steps), dims[position] // parts).reshape((-1,) + (1,) * (len(dims) - position - 1))

    gain = one(*split[0])
    for cut in split[1:]:
        gain = gain * one(*cut)
    return gain


def split_up(count, total, reach, skew):
    loads = [(1 << 20) // math.isqrt(grade ** skew) + 1 for grade in range(2, count + 1)]
    surplus, given = total - reach - (count - 1), [1] * (count - 1)
    while surplus > 0:
        candidates = [i for i in range(count - 1) if given[i] < reach]
        whole, budget = sum([loads[i] for i in candidates]), surplus
        for i in candidates:
            extra = min(reach - given[i], max(1, budget * loads[i] // whole), surplus)
            given[i] = given[i] + extra
            surplus = surplus - extra
    return np.array([reach] + given)


def ragged_sizes(stream_key, amount, total, reach, skew):
    if amount == 2:
        one = jax.random.randint(stream_key, (), max(1, total - reach), min(reach, total - 1) + 1)
        return jnp.stack([one, total - one])
    sizes = jnp.asarray(split_up(amount, total, reach, skew), jnp.int32)
    twos = (amount - 1) // 2
    donor, receiver = sizes[1:1 + 2 * twos:2], sizes[2:2 + 2 * twos:2]
    room = jnp.minimum(donor - 1, reach - receiver)
    shifted = jax.random.randint(jax.random.fold_in(stream_key, 1), (twos,), 0, 1 << 20) % (room + 1)
    sizes = sizes.at[1:1 + 2 * twos:2].set(donor - shifted).at[2:2 + 2 * twos:2].set(receiver + shifted)
    return sizes[jax.random.permutation(jax.random.fold_in(stream_key, 2), amount)]


def bell_draw(own_key, dims, scale, limit, split=(), kind=jnp.bfloat16):
    factor_of = shard_levels(own_key, dims, split, -0.22, 0.18) if split else 1.0
    array = jax.random.normal(own_key, dims, jnp.float32) * scale * factor_of
    return jnp.minimum(jnp.maximum(array, -limit), limit).astype(kind)


def setup_inputs(seed: int = 0) -> dict:
    keys = jax.random.split(jax.random.key(seed), 8)
    return {
        "slates": bell_draw(keys[0], (N_GRP, NC, D), 1.0, 6.0, ((0, 8), (1, 4))),
        "owner": jax.random.randint(keys[1], (1,), 0, N_GRP).astype(jnp.int32),
        "hist_keys": bell_draw(keys[2], (USERS, HIST, D), 1.0, 6.0, ((0, 8), (1, 4))),
        "hist_values": bell_draw(keys[3], (USERS, HIST, D), 1.0, 6.0, ((0, 8), (1, 4))),
        "lengths": ragged_sizes(keys[4], USERS, USERS * HIST // 2, HIST, 1).astype(jnp.int32),
        "proj_weight": bell_draw(keys[5], (D, 4, D), D ** -0.5, 0.1875, ((2, 4),)),
        "out_weight": bell_draw(keys[6], (D, D), D ** -0.5, 0.1875),
    }


def reference(slates, owner, hist_keys, hist_values, lengths, proj_weight, out_weight):
    slate = lax.dynamic_index_in_dim(slates, owner[0], 0, keepdims=False)
    projected = jnp.einsum('nd,dpc->npc', slate.astype(jnp.float32), proj_weight.astype(jnp.float32)).astype(jnp.bfloat16)
    head_size = D // H
    score_scale = 1.0 / math.sqrt(head_size)
    gate_in = projected[:, 0].astype(jnp.float32)
    query_heads = projected[:, 1].astype(jnp.float32).reshape(NC, H, head_size)
    self_keys = projected[:, 2].astype(jnp.float32).reshape(NC, H, head_size)
    self_values = projected[:, 3].astype(jnp.float32).reshape(NC, H, head_size)
    self_weight = jax.nn.silu(lax.optimization_barrier(jnp.sum(query_heads * self_keys, axis=-1)) * score_scale)
    self_term = (self_weight[:, :, None] * self_values).reshape(NC, D)
    positions = jnp.arange(HIST, dtype=jnp.int32)
    block_rows = math.gcd(NC, 512)
    query_blocks = query_heads.reshape(NC // block_rows, block_rows, H, head_size)
    slate_float = slate.astype(jnp.float32)

    def one_user(packed):
        key_rows, value_rows, length_one = packed
        visible = (positions < length_one).astype(jnp.float32)
        divisor = length_one.astype(jnp.float32) + 1.0
        key_heads = key_rows.astype(jnp.float32).reshape(HIST, H, head_size)
        value_heads = value_rows.astype(jnp.float32).reshape(HIST, H, head_size)

        def one_block(query_block):
            scores = jnp.einsum('bhe,khe->hbk', query_block, key_heads) * score_scale
            weights_bf = lax.optimization_barrier((jax.nn.silu(scores) * visible / divisor).astype(jnp.bfloat16))
            return jnp.einsum('hbk,khe->bhe', weights_bf.astype(jnp.float32), value_heads).reshape(block_rows, D)
        history = lax.map(one_block, query_blocks).reshape(NC, D)
        attended = history + self_term / divisor
        average = lax.optimization_barrier(jnp.mean(attended, axis=-1, keepdims=True))
        variance = lax.optimization_barrier(jnp.mean((attended - average) ** 2, axis=-1, keepdims=True))
        normed = (attended - average) * lax.rsqrt(variance + 1e-05)
        gated = (normed * jax.nn.silu(gate_in)).astype(jnp.bfloat16)
        mixed = jnp.dot(gated, out_weight, preferred_element_type=jnp.float32) + slate_float
        return mixed.astype(jnp.bfloat16)
    return lax.map(one_user, (hist_keys, hist_values, lengths))
```

```python
import functools
import math

import jax
import jax.numpy as jnp
from jax import lax
from jax.experimental import pallas as pl
from jax.experimental.pallas import tpu as pltpu
from jax.sharding import PartitionSpec as P

H = 16
BF = jnp.bfloat16
F32 = jnp.float32
VMEM_BYTES = 48 * 1024 * 1024


def head_mask(h, head_size, shape):
    lane_head = lax.broadcasted_iota(jnp.int32, shape, 1) // head_size
    return jnp.where(lane_head == h, 1.0, 0.0).astype(BF)


def half_silu(s):
    return s + s * jnp.tanh(s)


def attend_kernel(user, n_seq, head_size, tb, meta, proj, hk, hv, *rest):
    pieces = rest[: n_seq - 1]
    out, kst, vst, kbd, vbd, acc, sems = rest[n_seq - 1 :]
    tl = hk.shape[1]
    width = kst.shape[1]
    nh = width // head_size
    length = meta[user]
    me = meta[meta.shape[0] - 1]
    blocks = (length + tb - 1) // tb

    @pl.when(pl.program_id(0) == 0)
    def _():
        copies = []
        cols = pl.ds(0 if hk.shape[2] == width else pl.multiple_of(me * width, width), width)
        own = pl.ds(pl.multiple_of(me * tl, tl), tl)
        copies.append(pltpu.make_async_copy(hk.at[user, :, cols], kst.at[own], sems.at[0]))
        copies.append(pltpu.make_async_copy(hv.at[user, :, cols], vst.at[own], sems.at[1]))
        for j in range(1, n_seq):
            rows = pl.ds(pl.multiple_of(jnp.bitwise_xor(me, j) * tl, tl), tl)
            piece = pieces[j - 1]
            copies.append(
                pltpu.make_async_copy(piece.at[0, user], kst.at[rows], sems.at[2 * j])
            )
            copies.append(
                pltpu.make_async_copy(piece.at[1, user], vst.at[rows], sems.at[2 * j + 1])
            )
        for c in copies:
            c.start()
        for c in copies:
            c.wait()

        def expand(b, carry):
            src = pl.ds(pl.multiple_of(b * tb, tb), tb)
            k = kst[src, :]
            pos = b * tb + lax.broadcasted_iota(jnp.int32, (tb, width), 0)
            v = vst[src, :] * jnp.where(pos < length, 1.0, 0.0).astype(BF)
            for h in range(nh):
                m = head_mask(h, head_size, (tb, width))
                dst = pl.ds(pl.multiple_of((b * nh + h) * tb, tb), tb)
                kbd[dst, :] = k * m
                vbd[dst, :] = v * m
            return carry

        lax.fori_loop(0, blocks, expand, 0)

    scale = 0.5 / math.sqrt(head_size)
    q = proj[1]
    qs = q * jnp.asarray(scale, BF)
    prod = q.astype(F32) * proj[2].astype(F32)
    hi = prod.astype(BF)
    lo = (prod - hi.astype(F32)).astype(BF)
    row_head = lax.broadcasted_iota(jnp.int32, (width, width), 0) // head_size
    col_head = lax.broadcasted_iota(jnp.int32, (width, width), 1) // head_size
    same = jnp.where(row_head == col_head, 1.0, 0.0).astype(BF)
    dots = jnp.dot(hi, same, preferred_element_type=F32) + jnp.dot(
        lo, same, preferred_element_type=F32
    )
    acc[...] = half_silu(dots * scale) * proj[3].astype(F32)

    def step(b, carry):
        total = None
        for h in range(nh):
            rows = pl.ds(pl.multiple_of((b * nh + h) * tb, tb), tb)
            s = lax.dot_general(
                qs, kbd[rows, :], (((1,), (1,)), ((), ())), preferred_element_type=F32
            )
            w = half_silu(s).astype(BF)
            part = jnp.dot(w, vbd[rows, :], preferred_element_type=F32)
            total = part if total is None else total + part
        acc[...] += total
        return carry

    lax.fori_loop(0, blocks, step, 0)
    divisor = length.astype(F32) + 1.0
    out[...] = (acc[...] / divisor).astype(BF)


def attend(user, meta, proj, hk, hv, pieces, n_seq, head_size):
    _, n, width = proj.shape
    tl = hk.shape[1]
    t = tl * n_seq
    tb = math.gcd(t, 256)
    nh = width // head_size
    nb = math.gcd(n, 512)
    anyspec = pl.BlockSpec(memory_space=pl.ANY)
    return pl.pallas_call(
        functools.partial(attend_kernel, user, n_seq, head_size, tb),
        grid_spec=pltpu.PrefetchScalarGridSpec(
            num_scalar_prefetch=1,
            grid=(n // nb,),
            in_specs=[pl.BlockSpec((4, nb, width), lambda i, m: (0, i, 0))]
            + [anyspec] * (2 + len(pieces)),
            out_specs=pl.BlockSpec((nb, width), lambda i, m: (i, 0)),
            scratch_shapes=[
                pltpu.VMEM((t, width), BF),
                pltpu.VMEM((t, width), BF),
                pltpu.VMEM((t * nh, width), BF),
                pltpu.VMEM((t * nh, width), BF),
                pltpu.VMEM((nb, width), F32),
                pltpu.SemaphoreType.DMA((2 * n_seq,)),
            ],
        ),
        out_shape=jax.ShapeDtypeStruct((n, width), BF),
        compiler_params=pltpu.CompilerParams(
            vmem_limit_bytes=VMEM_BYTES, dimension_semantics=("arbitrary",)
        ),
        cost_estimate=pl.CostEstimate(
            flops=4 * n * t * nh * width, bytes_accessed=8 * n * width, transcendentals=n * t * nh
        ),
        name=f"attend_user{user}",
    )(meta, proj, hk, hv, *pieces)


def finish_kernel(n_seq, meta, own_att, own_gate, slate, ow, *rest):
    att_pieces = (own_att,) + rest[: n_seq - 1]
    gate_pieces = rest[n_seq - 1 : 2 * (n_seq - 1)]
    out = rest[-1]
    me = meta[meta.shape[0] - 1]
    rows, width = own_att.shape
    d = ow.shape[0]
    att = [a[...].astype(F32) for a in att_pieces]
    gates = [own_gate[0].astype(F32)] + [g[...].astype(F32) for g in gate_pieces]
    mean = sum(jnp.sum(a, axis=-1, keepdims=True) for a in att) * (1.0 / d)
    cent = [a - mean for a in att]
    var = sum(jnp.sum(c * c, axis=-1, keepdims=True) for c in cent) * (1.0 / d)
    inv = lax.rsqrt(var + 1e-05)
    total = slate[...].astype(F32)
    for j in range(n_seq):
        g = gates[j]
        half = 0.5 * g
        gated = (cent[j] * inv * half_silu(half)).astype(BF)
        src = pl.ds(pl.multiple_of(jnp.bitwise_xor(me, j) * width, width), width)
        total = total + jnp.dot(gated, ow[src, :], preferred_element_type=F32)
    out[0] = total.astype(BF)


def finish(user, users, meta, att, proj, slate, ow, att_pieces, gate_pieces, prior):
    n, width = att.shape
    d = ow.shape[0]
    n_seq = d // width
    rows = n // n_seq
    nb = math.gcd(rows, 256)
    steps = rows // nb

    def own(i, m):
        return m[m.shape[0] - 1] * steps + i

    piece = pl.BlockSpec((nb, width), lambda i, m: (i, 0))
    in_specs = [
        pl.BlockSpec((nb, width), lambda i, m: (own(i, m), 0)),
        pl.BlockSpec((1, nb, width), lambda i, m: (0, own(i, m), 0)),
        pl.BlockSpec((nb, d), lambda i, m: (own(i, m), 0)),
        pl.BlockSpec((d, d), lambda i, m: (0, 0)),
    ] + [piece] * (2 * (n_seq - 1))
    args = [meta, att, proj, slate, ow, *att_pieces, *gate_pieces]
    aliases = {}
    if prior is not None:
        in_specs.append(pl.BlockSpec(memory_space=pl.ANY))
        aliases = {len(args): 0}
        args.append(prior)
    return pl.pallas_call(
        functools.partial(finish_kernel, n_seq),
        grid_spec=pltpu.PrefetchScalarGridSpec(
            num_scalar_prefetch=1,
            grid=(steps,),
            in_specs=in_specs,
            out_specs=pl.BlockSpec((1, nb, d), lambda i, m: (user, i, 0)),
        ),
        out_shape=jax.ShapeDtypeStruct((users, rows, d), BF),
        input_output_aliases=aliases,
        compiler_params=pltpu.CompilerParams(
            vmem_limit_bytes=VMEM_BYTES, dimension_semantics=("arbitrary",)
        ),
        cost_estimate=pl.CostEstimate(
            flops=2 * rows * d * d, bytes_accessed=4 * rows * d + 2 * d * d, transcendentals=rows * d
        ),
        name=f"finish_user{user}",
    )(*args)


def local(slates, owner, hist_keys, hist_values, lengths, proj_weight, out_weight):
    n_seq = lax.axis_size("seq")
    me = lax.axis_index("seq")
    users = hist_keys.shape[0]
    d = slates.shape[2]
    head_size = d // H
    width = proj_weight.shape[2]
    meta = jnp.concatenate([lengths, me[None].astype(jnp.int32)])

    def swap(x, j):
        return lax.ppermute(x, "seq", [(s, s ^ j) for s in range(n_seq)])

    pieces = []
    for j in range(1, n_seq):
        start = (me ^ j) * width
        send = jnp.stack(
            [
                lax.dynamic_slice_in_dim(hist_keys, start, width, 2),
                lax.dynamic_slice_in_dim(hist_values, start, width, 2),
            ]
        )
        pieces.append(swap(send, j))

    own_keys, own_values = hist_keys, hist_values
    if width % 128:
        own_keys = lax.dynamic_slice_in_dim(hist_keys, me * width, width, 2)
        own_values = lax.dynamic_slice_in_dim(hist_values, me * width, width, 2)

    mine = lax.axis_index("grp") == owner[0]
    masked = jnp.where(mine, slates[0], jnp.zeros_like(slates[0]))
    part = lax.psum_scatter(masked, "grp", scatter_dimension=0, tiled=True)
    slate = lax.all_gather(part, ("seq", "grp"), axis=0, tiled=True)
    rows = slate.shape[0] // n_seq

    proj = jnp.einsum("nd,dpc->pnc", slate, proj_weight, preferred_element_type=F32).astype(BF)

    def to_rows(x):
        return [
            swap(lax.dynamic_slice_in_dim(x, (me ^ j) * rows, rows, 0), j)
            for j in range(1, n_seq)
        ]

    gate_pieces = to_rows(proj[0])
    out = None
    for u in range(users):
        att = attend(u, meta, proj, own_keys, own_values, pieces, n_seq, head_size)
        out = finish(
            u, users, meta, att, proj, slate, out_weight, to_rows(att), gate_pieces, out
        )
    return out


def solution(mesh):
    return jax.shard_map(
        local,
        mesh=mesh,
        in_specs=(
            P("grp", "seq", None),
            P(),
            P("grp", "seq", None),
            P("grp", "seq", None),
            P("grp"),
            P(None, None, "seq"),
            P(),
        ),
        out_specs=P("grp", "seq", None),
        check_vma=False,
    )
```

```python
import functools
import math

import jax
import jax.numpy as jnp
from jax import lax
from jax.experimental import pallas as pl
from jax.experimental.pallas import tpu as pltpu
from jax.sharding import PartitionSpec as P

H = 16
BF = jnp.bfloat16
F32 = jnp.float32
VMEM_BYTES = 48 * 1024 * 1024


def head_mask(h, head_size, shape):
    lane_head = lax.broadcasted_iota(jnp.int32, shape, 1) // head_size
    return jnp.where(lane_head == h, 1.0, 0.0).astype(BF)


def half_silu(s):
    return s + s * jnp.tanh(s)


def attend_kernel(user, n_seq, head_size, tb, meta, proj, hk, hv, *rest):
    pieces = rest[: n_seq - 1]
    out, kst, vst, kbd, vbd, acc, sems = rest[n_seq - 1 :]
    tl = hk.shape[1]
    width = kst.shape[1]
    nh = width // head_size
    length = meta[user]
    me = meta[meta.shape[0] - 1]
    blocks = (length + tb - 1) // tb

    @pl.when(pl.program_id(0) == 0)
    def _():
        copies = []
        cols = pl.ds(0 if hk.shape[2] == width else pl.multiple_of(me * width, width), width)
        own = pl.ds(pl.multiple_of(me * tl, tl), tl)
        copies.append(pltpu.make_async_copy(hk.at[user, :, cols], kst.at[own], sems.at[0]))
        copies.append(pltpu.make_async_copy(hv.at[user, :, cols], vst.at[own], sems.at[1]))
        for j in range(1, n_seq):
            rows = pl.ds(pl.multiple_of(jnp.bitwise_xor(me, j) * tl, tl), tl)
            piece = pieces[j - 1]
            copies.append(
                pltpu.make_async_copy(piece.at[0, user], kst.at[rows], sems.at[2 * j])
            )
            copies.append(
                pltpu.make_async_copy(piece.at[1, user], vst.at[rows], sems.at[2 * j + 1])
            )
        for c in copies:
            c.start()
        for c in copies:
            c.wait()

        def expand(b, carry):
            src = pl.ds(pl.multiple_of(b * tb, tb), tb)
            k = kst[src, :]
            pos = b * tb + lax.broadcasted_iota(jnp.int32, (tb, width), 0)
            v = vst[src, :] * jnp.where(pos < length, 1.0, 0.0).astype(BF)
            for h in range(nh):
                m = head_mask(h, head_size, (tb, width))
                dst = pl.ds(pl.multiple_of((b * nh + h) * tb, tb), tb)
                kbd[dst, :] = k * m
                vbd[dst, :] = v * m
            return carry

        lax.fori_loop(0, blocks, expand, 0)

    scale = 0.5 / math.sqrt(head_size)
    q = proj[1]
    qs = q * jnp.asarray(scale, BF)
    prod = q.astype(F32) * proj[2].astype(F32)
    hi = prod.astype(BF)
    lo = (prod - hi.astype(F32)).astype(BF)
    row_head = lax.broadcasted_iota(jnp.int32, (width, width), 0) // head_size
    col_head = lax.broadcasted_iota(jnp.int32, (width, width), 1) // head_size
    same = jnp.where(row_head == col_head, 1.0, 0.0).astype(BF)
    dots = jnp.dot(hi, same, preferred_element_type=F32) + jnp.dot(
        lo, same, preferred_element_type=F32
    )
    acc[...] = half_silu(dots * scale) * proj[3].astype(F32)

    def step(b, carry):
        total = None
        for h in range(nh):
            rows = pl.ds(pl.multiple_of((b * nh + h) * tb, tb), tb)
            s = lax.dot_general(
                qs, kbd[rows, :], (((1,), (1,)), ((), ())), preferred_element_type=F32
            )
            w = half_silu(s).astype(BF)
            part = jnp.dot(w, vbd[rows, :], preferred_element_type=F32)
            total = part if total is None else total + part
        acc[...] += total
        return carry

    lax.fori_loop(0, blocks, step, 0)
    divisor = length.astype(F32) + 1.0
    out[...] = (acc[...] / divisor).astype(BF)


def attend(user, meta, proj, hk, hv, pieces, n_seq, head_size):
    _, n, width = proj.shape
    tl = hk.shape[1]
    t = tl * n_seq
    tb = math.gcd(t, 256)
    nh = width // head_size
    nb = math.gcd(n, 512)
    anyspec = pl.BlockSpec(memory_space=pl.ANY)
    return pl.pallas_call(
        functools.partial(attend_kernel, user, n_seq, head_size, tb),
        grid_spec=pltpu.PrefetchScalarGridSpec(
            num_scalar_prefetch=1,
            grid=(n // nb,),
            in_specs=[pl.BlockSpec((4, nb, width), lambda i, m: (0, i, 0))]
            + [anyspec] * (2 + len(pieces)),
            out_specs=pl.BlockSpec((nb, width), lambda i, m: (i, 0)),
            scratch_shapes=[
                pltpu.VMEM((t, width), BF),
                pltpu.VMEM((t, width), BF),
                pltpu.VMEM((t * nh, width), BF),
                pltpu.VMEM((t * nh, width), BF),
                pltpu.VMEM((nb, width), F32),
                pltpu.SemaphoreType.DMA((2 * n_seq,)),
            ],
        ),
        out_shape=jax.ShapeDtypeStruct((n, width), BF),
        compiler_params=pltpu.CompilerParams(
            vmem_limit_bytes=VMEM_BYTES, dimension_semantics=("arbitrary",)
        ),
        cost_estimate=pl.CostEstimate(
            flops=4 * n * t * nh * width, bytes_accessed=8 * n * width, transcendentals=n * t * nh
        ),
        name=f"attend_user{user}",
    )(meta, proj, hk, hv, *pieces)


def finish_kernel(n_seq, meta, own_att, own_gate, slate, ow, *rest):
    att_pieces = (own_att,) + rest[: n_seq - 1]
    gate_pieces = rest[n_seq - 1 : 2 * (n_seq - 1)]
    out = rest[-1]
    me = meta[meta.shape[0] - 1]
    rows, width = own_att.shape
    d = ow.shape[0]
    att = [a[...].astype(F32) for a in att_pieces]
    gates = [own_gate[0].astype(F32)] + [g[...].astype(F32) for g in gate_pieces]
    mean = sum(jnp.sum(a, axis=-1, keepdims=True) for a in att) * (1.0 / d)
    cent = [a - mean for a in att]
    var = sum(jnp.sum(c * c, axis=-1, keepdims=True) for c in cent) * (1.0 / d)
    inv = lax.rsqrt(var + 1e-05)
    total = slate[...].astype(F32)
    for j in range(n_seq):
        g = gates[j]
        half = 0.5 * g
        gated = (cent[j] * inv * half_silu(half)).astype(BF)
        src = pl.ds(pl.multiple_of(jnp.bitwise_xor(me, j) * width, width), width)
        total = total + jnp.dot(gated, ow[src, :], preferred_element_type=F32)
    out[0] = total.astype(BF)


def finish(user, users, meta, att, proj, slate, ow, att_pieces, gate_pieces, prior):
    n, width = att.shape
    d = ow.shape[0]
    n_seq = d // width
    rows = n // n_seq
    nb = math.gcd(rows // 2, 256)
    steps = rows // nb

    def place(i, m):
        return lax.rem(i + m[m.shape[0] - 2] * (steps // 2), steps)

    piece = pl.BlockSpec((nb, width), lambda i, m: (i, 0))
    in_specs = [
        pl.BlockSpec((nb, width), lambda i, m: (i, 0)),
        pl.BlockSpec((1, nb, width), lambda i, m: (0, i, 0)),
        pl.BlockSpec((nb, d), lambda i, m: (i, 0)),
        pl.BlockSpec((d, d), lambda i, m: (0, 0)),
    ] + [piece] * (2 * (n_seq - 1))
    args = [meta, att, proj, slate, ow, *att_pieces, *gate_pieces]
    aliases = {}
    if prior is not None:
        in_specs.append(pl.BlockSpec(memory_space=pl.ANY))
        aliases = {len(args): 0}
        args.append(prior)
    return pl.pallas_call(
        functools.partial(finish_kernel, n_seq),
        grid_spec=pltpu.PrefetchScalarGridSpec(
            num_scalar_prefetch=1,
            grid=(steps,),
            in_specs=in_specs,
            out_specs=pl.BlockSpec((1, nb, d), lambda i, m: (user, place(i, m), 0)),
        ),
        out_shape=jax.ShapeDtypeStruct((users, rows, d), BF),
        input_output_aliases=aliases,
        compiler_params=pltpu.CompilerParams(
            vmem_limit_bytes=VMEM_BYTES, dimension_semantics=("arbitrary",)
        ),
        cost_estimate=pl.CostEstimate(
            flops=2 * rows * d * d, bytes_accessed=4 * rows * d + 2 * d * d, transcendentals=rows * d
        ),
        name=f"finish_user{user}",
    )(*args)


def swap(x, j, axis="seq"):
    return lax.ppermute(x, axis, [(s, s ^ j) for s in range(lax.axis_size(axis))])


def spread_slate(own, owner, pieces):
    n_grp = lax.axis_size("grp")
    n_seq = lax.axis_size("seq")
    g = lax.axis_index("grp")
    z, y, z0, y0 = g // 2, g % 2, owner // 2, owner % 2
    half = own.shape[0] // 2
    quarter = half // 2
    mine = jnp.where(y == y0, own[:half], swap(own[half:], 1, "grp"))
    here = z == z0
    up = [(s, s + 2) for s in range(n_grp - 2)]
    down = [(s + 2, s) for s in range(n_grp - 2)]
    parts = [mine[c * quarter : (c + 1) * quarter] for c in range(2)]
    slots = n_grp // 2
    order = [j - 1 for j in range(2, n_seq, 2)] + [j - 1 for j in range(1, n_seq, 2)]
    order = [order[0]] + [j for j in range(n_seq - 1) if j != order[0] and j % 2 == 0 and j] + [
        j for j in order[1:] if j % 2 or j == 0
    ]
    pieces = list(pieces)
    right, left, got = parts[0], parts[0], []
    for slot in range(slots):
        right = lax.ppermute(right, "grp", up)
        left = lax.ppermute(left, "grp", down)
        if slot:
            mine_now = order[slot - 1 :] if slot == slots - 1 else order[slot - 1 : slot]
            tied = [pieces[i] for i in mine_now]
            (right, left, tied) = lax.optimization_barrier((right, left, tied))
            for i, p in zip(mine_now, tied):
                pieces[i] = p
        got.append(jnp.where(z > z0, right, left))
        right = jnp.where(here, parts[1], right)
        left = jnp.where(here, parts[1], left)
    distance = jnp.abs(z - z0)
    whole = lax.dynamic_slice_in_dim(
        jnp.concatenate(got), jnp.maximum(distance - 1, 0) * quarter, half, 0
    )
    whole = jnp.where(here, mine, whole)
    chunks = [whole[:quarter], whole[quarter:]]
    blocks = {(0, 0): chunks, (0, 1): [swap(c, 1, "grp") for c in chunks]}
    for j in range(2, n_seq, 2):
        across = [swap(c, j) for c in chunks]
        blocks[(j, 0)] = across
        blocks[(j, 1)] = [swap(blocks[(0, 1)][0], j), swap(across[1], 1, "grp")]
    for j in range(0, n_seq, 2):
        for h in range(2):
            blocks[(j + 1, h)] = [swap(c, 1) for c in blocks[(j, h)]]
    order = [c for j in range(n_seq) for h in range(2) for c in blocks[(j, h)]]
    return jnp.concatenate(order, axis=0), jnp.where(y == y0, 0, 1), pieces


def local(slates, owner, hist_keys, hist_values, lengths, proj_weight, out_weight):
    n_seq = lax.axis_size("seq")
    me = lax.axis_index("seq")
    users = hist_keys.shape[0]
    d = slates.shape[2]
    head_size = d // H
    width = proj_weight.shape[2]
    pieces = []
    for j in range(1, n_seq):
        start = (me ^ j) * width
        send = jnp.stack(
            [
                lax.dynamic_slice_in_dim(hist_keys, start, width, 2),
                lax.dynamic_slice_in_dim(hist_values, start, width, 2),
            ]
        )
        pieces.append(swap(send, j))

    own_keys, own_values = hist_keys, hist_values
    if width % 128:
        own_keys = lax.dynamic_slice_in_dim(hist_keys, me * width, width, 2)
        own_values = lax.dynamic_slice_in_dim(hist_values, me * width, width, 2)

    slate, flip, pieces = spread_slate(slates[0], owner[0], pieces)
    rows = slate.shape[0] // n_seq
    meta = jnp.concatenate([lengths, jnp.stack([flip, me]).astype(jnp.int32)])

    proj = jnp.einsum("nd,dpc->pnc", slate, proj_weight, preferred_element_type=F32).astype(BF)

    def to_rows(x):
        return [
            swap(x[j * rows : (j + 1) * rows], j)
            for j in range(1, n_seq)
        ]

    gate_pieces = to_rows(proj[0])
    out = None
    for u in range(users):
        att = attend(u, meta, proj, own_keys, own_values, pieces, n_seq, head_size)
        out = finish(
            u, users, meta, att, proj, slate, out_weight, to_rows(att), gate_pieces, out
        )
    return out


def solution(mesh):
    return jax.shard_map(
        local,
        mesh=mesh,
        in_specs=(
            P("grp", "seq", None),
            P(),
            P("grp", "seq", None),
            P("grp", "seq", None),
            P("grp"),
            P(None, None, "seq"),
            P(),
        ),
        out_specs=P("grp", "seq", None),
        check_vma=False,
    )
```

```python
import functools
import math

import jax
import jax.numpy as jnp
from jax import lax
from jax.experimental import pallas as pl
from jax.experimental.pallas import tpu as pltpu
from jax.sharding import PartitionSpec as P

H = 16
BF = jnp.bfloat16
F32 = jnp.float32
VMEM_BYTES = 48 * 1024 * 1024


def head_mask(h, head_size, shape):
    lane_head = lax.broadcasted_iota(jnp.int32, shape, 1) // head_size
    return jnp.where(lane_head == h, 1.0, 0.0).astype(BF)


def half_silu(s):
    return s + s * jnp.tanh(s)


def gate_scores(s):
    return half_silu(s).astype(BF)


def attend_kernel(user, n_seq, head_size, tb, meta, proj, hk, hv, *rest):
    pieces = rest[: n_seq - 1]
    out, kst, vst, kbd, vbd, acc, sems = rest[n_seq - 1 :]
    tl = hk.shape[1]
    width = kst.shape[1]
    nh = width // head_size
    length = meta[user]
    me = meta[meta.shape[0] - 1]
    blocks = (length + tb - 1) // tb

    @pl.when(pl.program_id(0) == 0)
    def _():
        copies = []
        cols = pl.ds(0 if hk.shape[2] == width else pl.multiple_of(me * width, width), width)
        own = pl.ds(pl.multiple_of(me * tl, tl), tl)
        copies.append(pltpu.make_async_copy(hk.at[user, :, cols], kst.at[own], sems.at[0]))
        copies.append(pltpu.make_async_copy(hv.at[user, :, cols], vst.at[own], sems.at[1]))
        for j in range(1, n_seq):
            rows = pl.ds(pl.multiple_of(jnp.bitwise_xor(me, j) * tl, tl), tl)
            piece = pieces[j - 1]
            copies.append(
                pltpu.make_async_copy(piece.at[0, user], kst.at[rows], sems.at[2 * j])
            )
            copies.append(
                pltpu.make_async_copy(piece.at[1, user], vst.at[rows], sems.at[2 * j + 1])
            )
        for c in copies:
            c.start()
        for c in copies:
            c.wait()

        def expand(b, carry):
            src = pl.ds(pl.multiple_of(b * tb, tb), tb)
            k = kst[src, :]
            pos = b * tb + lax.broadcasted_iota(jnp.int32, (tb, width), 0)
            v = vst[src, :] * jnp.where(pos < length, 1.0, 0.0).astype(BF)
            for h in range(nh):
                m = head_mask(h, head_size, (tb, width))
                dst = pl.ds(pl.multiple_of((b * nh + h) * tb, tb), tb)
                kbd[dst, :] = k * m
                vbd[dst, :] = v * m
            return carry

        lax.fori_loop(0, blocks, expand, 0)

    scale = 0.5 / math.sqrt(head_size)
    q = proj[1]
    qs = q * jnp.asarray(scale, BF)
    prod = q.astype(F32) * proj[2].astype(F32)
    hi = prod.astype(BF)
    lo = (prod - hi.astype(F32)).astype(BF)
    row_head = lax.broadcasted_iota(jnp.int32, (width, width), 0) // head_size
    col_head = lax.broadcasted_iota(jnp.int32, (width, width), 1) // head_size
    same = jnp.where(row_head == col_head, 1.0, 0.0).astype(BF)
    dots = jnp.dot(hi, same, preferred_element_type=F32) + jnp.dot(
        lo, same, preferred_element_type=F32
    )
    acc[...] = half_silu(dots * scale) * proj[3].astype(F32)

    def step(b, carry):
        ws = []
        for h in range(nh):
            rows = pl.ds(pl.multiple_of((b * nh + h) * tb, tb), tb)
            s = lax.dot_general(
                qs, kbd[rows, :], (((1,), (1,)), ((), ())), preferred_element_type=F32
            )
            ws.append(gate_scores(s))
        rows = pl.ds(pl.multiple_of(b * nh * tb, tb), nh * tb)
        acc[...] += jnp.dot(
            jnp.concatenate(ws, axis=1), vbd[rows, :], preferred_element_type=F32
        )
        return carry

    lax.fori_loop(0, blocks, step, 0)
    divisor = length.astype(F32) + 1.0
    out[...] = (acc[...] / divisor).astype(BF)


def attend(user, meta, proj, hk, hv, pieces, n_seq, head_size):
    _, n, width = proj.shape
    tl = hk.shape[1]
    t = tl * n_seq
    tb = math.gcd(t, 256)
    nh = width // head_size
    nb = math.gcd(n, 1024)
    anyspec = pl.BlockSpec(memory_space=pl.ANY)
    return pl.pallas_call(
        functools.partial(attend_kernel, user, n_seq, head_size, tb),
        grid_spec=pltpu.PrefetchScalarGridSpec(
            num_scalar_prefetch=1,
            grid=(n // nb,),
            in_specs=[pl.BlockSpec((4, nb, width), lambda i, m: (0, i, 0))]
            + [anyspec] * (2 + len(pieces)),
            out_specs=pl.BlockSpec((nb, width), lambda i, m: (i, 0)),
            scratch_shapes=[
                pltpu.VMEM((t, width), BF),
                pltpu.VMEM((t, width), BF),
                pltpu.VMEM((t * nh, width), BF),
                pltpu.VMEM((t * nh, width), BF),
                pltpu.VMEM((nb, width), F32),
                pltpu.SemaphoreType.DMA((2 * n_seq,)),
            ],
        ),
        out_shape=jax.ShapeDtypeStruct((n, width), BF),
        compiler_params=pltpu.CompilerParams(
            vmem_limit_bytes=VMEM_BYTES, dimension_semantics=("arbitrary",)
        ),
        cost_estimate=pl.CostEstimate(
            flops=4 * n * t * nh * width, bytes_accessed=8 * n * width, transcendentals=n * t * nh
        ),
        name=f"attend_user{user}",
    )(meta, proj, hk, hv, *pieces)


def finish_kernel(n_seq, meta, own_att, own_gate, slate, ow, *rest):
    att_pieces = (own_att,) + rest[: n_seq - 1]
    gate_pieces = rest[n_seq - 1 : 2 * (n_seq - 1)]
    out = rest[-1]
    me = meta[meta.shape[0] - 1]
    rows, width = own_att.shape
    d = ow.shape[0]
    att = [a[...].astype(F32) for a in att_pieces]
    gates = [own_gate[0].astype(F32)] + [g[...].astype(F32) for g in gate_pieces]
    mean = sum(jnp.sum(a, axis=-1, keepdims=True) for a in att) * (1.0 / d)
    cent = [a - mean for a in att]
    var = sum(jnp.sum(c * c, axis=-1, keepdims=True) for c in cent) * (1.0 / d)
    inv = lax.rsqrt(var + 1e-05)
    total = slate[...].astype(F32)
    for j in range(n_seq):
        g = gates[j]
        half = 0.5 * g
        gated = (cent[j] * inv * half_silu(half)).astype(BF)
        src = pl.ds(pl.multiple_of(jnp.bitwise_xor(me, j) * width, width), width)
        total = total + jnp.dot(gated, ow[src, :], preferred_element_type=F32)
    out[0] = total.astype(BF)


def finish(user, users, meta, att, proj, slate, ow, att_pieces, gate_pieces, prior):
    n, width = att.shape
    d = ow.shape[0]
    n_seq = d // width
    rows = n // n_seq
    nb = math.gcd(rows // 2, 256)
    steps = rows // nb

    def place(i, m):
        return lax.rem(i + m[m.shape[0] - 2] * (steps // 2), steps)

    piece = pl.BlockSpec((nb, width), lambda i, m: (i, 0))
    in_specs = [
        pl.BlockSpec((nb, width), lambda i, m: (i, 0)),
        pl.BlockSpec((1, nb, width), lambda i, m: (0, i, 0)),
        pl.BlockSpec((nb, d), lambda i, m: (i, 0)),
        pl.BlockSpec((d, d), lambda i, m: (0, 0)),
    ] + [piece] * (2 * (n_seq - 1))
    args = [meta, att, proj, slate, ow, *att_pieces, *gate_pieces]
    aliases = {}
    if prior is not None:
        in_specs.append(pl.BlockSpec(memory_space=pl.ANY))
        aliases = {len(args): 0}
        args.append(prior)
    return pl.pallas_call(
        functools.partial(finish_kernel, n_seq),
        grid_spec=pltpu.PrefetchScalarGridSpec(
            num_scalar_prefetch=1,
            grid=(steps,),
            in_specs=in_specs,
            out_specs=pl.BlockSpec((1, nb, d), lambda i, m: (user, place(i, m), 0)),
        ),
        out_shape=jax.ShapeDtypeStruct((users, rows, d), BF),
        input_output_aliases=aliases,
        compiler_params=pltpu.CompilerParams(
            vmem_limit_bytes=VMEM_BYTES, dimension_semantics=("arbitrary",)
        ),
        cost_estimate=pl.CostEstimate(
            flops=2 * rows * d * d, bytes_accessed=4 * rows * d + 2 * d * d, transcendentals=rows * d
        ),
        name=f"finish_user{user}",
    )(*args)


def swap(x, j, axis="seq"):
    return lax.ppermute(x, axis, [(s, s ^ j) for s in range(lax.axis_size(axis))])


def spread_slate(own, owner, pieces):
    n_grp = lax.axis_size("grp")
    n_seq = lax.axis_size("seq")
    g = lax.axis_index("grp")
    z, y, z0, y0 = g // 2, g % 2, owner // 2, owner % 2
    half = own.shape[0] // 2
    quarter = half // 2
    mine = jnp.where(y == y0, own[:half], swap(own[half:], 1, "grp"))
    here = z == z0
    up = [(s, s + 2) for s in range(n_grp - 2)]
    down = [(s + 2, s) for s in range(n_grp - 2)]
    parts = [mine[c * quarter : (c + 1) * quarter] for c in range(2)]
    slots = n_grp // 2
    order = [j - 1 for j in range(2, n_seq, 2)] + [j - 1 for j in range(1, n_seq, 2)]
    order = [order[0]] + [j for j in range(n_seq - 1) if j != order[0] and j % 2 == 0 and j] + [
        j for j in order[1:] if j % 2 or j == 0
    ]
    pieces = list(pieces)
    right, left, got = parts[0], parts[0], []
    for slot in range(slots):
        right = lax.ppermute(right, "grp", up)
        left = lax.ppermute(left, "grp", down)
        if slot:
            mine_now = order[slot - 1 :] if slot == slots - 1 else order[slot - 1 : slot]
            tied = [pieces[i] for i in mine_now]
            (right, left, tied) = lax.optimization_barrier((right, left, tied))
            for i, p in zip(mine_now, tied):
                pieces[i] = p
        got.append(jnp.where(z > z0, right, left))
        right = jnp.where(here, parts[1], right)
        left = jnp.where(here, parts[1], left)
    distance = jnp.abs(z - z0)
    whole = lax.dynamic_slice_in_dim(
        jnp.concatenate(got), jnp.maximum(distance - 1, 0) * quarter, half, 0
    )
    whole = jnp.where(here, mine, whole)
    chunks = [whole[:quarter], whole[quarter:]]
    blocks = {(0, 0): chunks, (0, 1): [swap(c, 1, "grp") for c in chunks]}
    for j in range(2, n_seq, 2):
        across = [swap(c, j) for c in chunks]
        blocks[(j, 0)] = across
        blocks[(j, 1)] = [swap(blocks[(0, 1)][0], j), swap(across[1], 1, "grp")]
    for j in range(0, n_seq, 2):
        for h in range(2):
            blocks[(j + 1, h)] = [swap(c, 1) for c in blocks[(j, h)]]
    order = [c for j in range(n_seq) for h in range(2) for c in blocks[(j, h)]]
    return order, jnp.where(y == y0, 0, 1), pieces


def project_kernel(count, per_seq, *refs):
    chunks, w, proj, own, rows = refs[:count], *refs[count:]
    r = chunks[0].shape[0]

    @pl.when(pl.program_id(0) == 0)
    def _():
        for c in range(count):
            rows[pl.ds(c * r, r), :] = chunks[c][...]
        own[...] = rows[pl.ds(0, per_seq * r), :]

    nb = math.gcd(count * r, 512)
    for i in range(count * r // nb):
        block = pl.ds(i * nb, nb)
        proj[0, block, :] = jnp.dot(
            rows[block, :], w[0], preferred_element_type=F32
        ).astype(BF)


def project(chunks, w, n_seq):
    count = len(chunks)
    r, d = chunks[0].shape
    width = w.shape[2]
    per_seq = count // n_seq
    return pl.pallas_call(
        functools.partial(project_kernel, count, per_seq),
        grid=(4,),
        in_specs=[pl.BlockSpec((r, d), lambda p: (0, 0))] * count
        + [pl.BlockSpec((1, d, width), lambda p: (p, 0, 0))],
        out_specs=[
            pl.BlockSpec((1, count * r, width), lambda p: (p, 0, 0)),
            pl.BlockSpec((per_seq * r, d), lambda p: (0, 0)),
        ],
        out_shape=[
            jax.ShapeDtypeStruct((4, count * r, width), BF),
            jax.ShapeDtypeStruct((per_seq * r, d), BF),
        ],
        scratch_shapes=[pltpu.VMEM((count * r, d), BF)],
        compiler_params=pltpu.CompilerParams(
            vmem_limit_bytes=VMEM_BYTES, dimension_semantics=("arbitrary",)
        ),
        cost_estimate=pl.CostEstimate(
            flops=8 * count * r * d * width, bytes_accessed=4 * count * r * d, transcendentals=0
        ),
        name="project",
    )(*chunks, w)


def local(slates, owner, hist_keys, hist_values, lengths, proj_weight, out_weight):
    n_seq = lax.axis_size("seq")
    me = lax.axis_index("seq")
    users = hist_keys.shape[0]
    d = slates.shape[2]
    head_size = d // H
    width = proj_weight.shape[2]
    pieces = []
    for j in range(1, n_seq):
        start = (me ^ j) * width
        send = jnp.stack(
            [
                lax.dynamic_slice_in_dim(hist_keys, start, width, 2),
                lax.dynamic_slice_in_dim(hist_values, start, width, 2),
            ]
        )
        pieces.append(swap(send, j))

    own_keys, own_values = hist_keys, hist_values
    if width % 128:
        own_keys = lax.dynamic_slice_in_dim(hist_keys, me * width, width, 2)
        own_values = lax.dynamic_slice_in_dim(hist_values, me * width, width, 2)

    chunks, flip, pieces = spread_slate(slates[0], owner[0], pieces)
    rows = slates.shape[1]
    meta = jnp.concatenate([lengths, jnp.stack([flip, me]).astype(jnp.int32)])

    proj, slate = project(chunks, jnp.transpose(proj_weight, (1, 0, 2)), n_seq)

    def to_rows(x):
        return [
            swap(x[j * rows : (j + 1) * rows], j)
            for j in range(1, n_seq)
        ]

    gate_pieces = to_rows(proj[0])
    out = None
    for u in range(users):
        att = attend(u, meta, proj, own_keys, own_values, pieces, n_seq, head_size)
        out = finish(
            u, users, meta, att, proj, slate, out_weight, to_rows(att), gate_pieces, out
        )
    return out


def solution(mesh):
    return jax.shard_map(
        local,
        mesh=mesh,
        in_specs=(
            P("grp", "seq", None),
            P(),
            P("grp", "seq", None),
            P("grp", "seq", None),
            P("grp"),
            P(None, None, "seq"),
            P(),
        ),
        out_specs=P("grp", "seq", None),
        check_vma=False,
    )
```
